32 devices in a mesh: parts: 2 (over x), gx: 16 (over z, y, core).
Axes of the slice: x: 2, y: 2, z: 4, core: 2. Of those that a mesh axis runs over, the one named last changes fastest.
Arguments:
- state: float32 [64, 512, 128], P(None, ('parts', 'gx')), parts along dimension 1, may hold values from -6 to 6
- cotangent: float32 [64, 512, 128], P(None, ('parts', 'gx')), parts along dimension 1, may hold values from -5 to 5
- kappa: float32 [512, 128], P(('parts', 'gx')), parts along dimension 0, may hold values from 0.04 to 0.2
- labels: int32 [512, 128], P(('parts', 'gx')), parts along dimension 0, may hold values from 0 to 3
- drift: float32 [64], replicated, may hold values from -0.6 to 0.6
- w_in: bfloat16 [4, 256, 64], replicated, may hold values from -0.75 to 0.75
- b_in: float32 [4, 256], replicated, may hold values from -3 to 3
- w_mid: bfloat16 [4, 256, 256], replicated, may hold values from -0.375 to 0.375
- b_mid: float32 [4, 256], replicated, may hold values from -3 to 3
- w_out: bfloat16 [4, 64, 256], replicated, may hold values from -0.375 to 0.375
- b_out: float32 [4, 64], replicated, may hold values from -3 to 3
Outputs:
- state_grad: float32 [64, 512, 128], P(None, ('parts', 'gx')), parts along dimension 1
- w_in_grad: float32 [8, 256, 64], P('parts'), parts along dimension 0
- b_in_grad: float32 [8, 256], P('parts'), parts along dimension 0
- w_mid_grad: float32 [8, 256, 256], P('parts'), parts along dimension 0
- b_mid_grad: float32 [8, 256], P('parts'), parts along dimension 0
- w_out_grad: float32 [8, 64, 256], P('parts'), parts along dimension 0
- b_out_grad: float32 [8, 64], P('parts'), parts along dimension 0
The draws below stay inside these ranges and needn't reach their ends.
There are 2 independent parts, one for each index of `parts`. The reference program is written for one: setup_inputs(seed, part) draws one part's arguments, and reference() takes and returns one part's arrays. A program takes and returns all parts, laid end to end along the dimension named above; an argument that names none is the same for every part. Nothing has to cross between parts.
All inputs are finite; a program needn't handle non-finite values.
Results may differ from the reference program's by a relative error of at most 0.011.
Values sent between devices are 32-bit elements; how exact they have to be, the bound alone decides.
A program may use at most 128 MiB of HBM per device.

```python
import math
import jax
import jax.numpy as jnp
from jax import lax

NZ = 64
HID = 256
EXPERTS = 4
NY = 128
NX = 256


def draw_cotangent(key, part):
    key = jax.random.fold_in(key, 5)
    noise_key, level_key = jax.random.split(key)
    x_ramp = 0.3 + 0.6 * jnp.arange(NX, dtype=jnp.float32)[None, :, None] / NX
    base_noise = jax.random.truncated_normal(noise_key, -4.0, 4.0, (NZ, NX, NY), jnp.float32)
    level_sign = jax.random.uniform(level_key, (NZ, 1, 1), jnp.float32, -1.0, 1.0)
    return base_noise + level_sign * x_ramp


def draw_labels(key, part):
    key = jax.random.fold_in(key, 11)
    return jax.random.randint(key, (NX, NY), 0, EXPERTS, dtype=jnp.int32)


def steps_of(key, dims, shards, least, high):
    loudness = 1.0
    for axis_at, parts in shards:
        steps = jax.random.uniform(jax.random.fold_in(jax.random.fold_in(key, 6), axis_at), (parts,), jnp.float32, least / len(shards), high / len(shards))
        loudness = loudness * jnp.repeat(jnp.exp(steps), dims[axis_at] // parts).reshape((-1,) + (1,) * (len(dims) - 1 - axis_at))
    return loudness


def gaussian(stream_key, extent, spread, limit, shards=(), held_as=jnp.bfloat16):
    gain = steps_of(stream_key, extent, shards, -0.22, 0.18) if shards else 1.0
    result = jax.random.normal(stream_key, extent, jnp.float32) * spread * gain
    return jnp.minimum(jnp.maximum(result, -limit), limit).astype(held_as)


def setup_inputs(seed: int = 0, part: int = 0) -> dict:
    splits = jax.random.split(jax.random.key(seed), 12)
    part_keys = jax.random.split(jax.random.fold_in(splits[11], part), 12)
    return {
        "state": gaussian(part_keys[0], (NZ, NX, NY), 1.0, 6.0, ((1, 16),), jnp.float32),
        "cotangent": draw_cotangent(jax.random.fold_in(jax.random.fold_in(splits[11], part), 71), part),
        "kappa": jnp.clip(jnp.exp(math.log(0.2) - 1.609438 * jax.random.uniform(part_keys[2], (NX, NY), jnp.float32) ** steps_of(part_keys[2], (NX, NY), ((0, 16),), -0.2, 0.2)), 0.04, 0.2),
        "labels": draw_labels(jax.random.fold_in(jax.random.fold_in(splits[11], part), 71), part),
        "drift": jnp.clip(jax.random.uniform(splits[4], (NZ,), jnp.float32, -0.6, 0.6), -0.6, 0.6),
        "w_in": gaussian(splits[5], (EXPERTS, HID, NZ), NZ ** -0.5, 0.75),
        "b_in": gaussian(splits[6], (EXPERTS, HID), 0.5, 3.0, (), jnp.float32),
        "w_mid": gaussian(splits[7], (EXPERTS, HID, HID), HID ** -0.5, 0.375),
        "b_mid": gaussian(splits[8], (EXPERTS, HID), 0.5, 3.0, (), jnp.float32),
        "w_out": gaussian(splits[9], (EXPERTS, NZ, HID), HID ** -0.5, 0.375),
        "b_out": gaussian(splits[10], (EXPERTS, NZ), 0.5, 3.0, (), jnp.float32),
    }


step_size = 0.8
gelu_coef = 0.7978845608028654


def gelu_tanh(value):
    inner = gelu_coef * (value + 0.044715 * value * value * value)
    return 0.5 * value * (1.0 + jnp.tanh(inner))


def gelu_slope(value):
    inner = gelu_coef * (value + 0.044715 * value * value * value)
    tangent = jnp.tanh(inner)
    return 0.5 * (1.0 + tangent) + 0.5 * value * (1.0 - tangent * tangent) * gelu_coef * (1.0 + 3.0 * 0.044715 * value * value)


def expert_forward(columns, weights):
    w_in, b_in, w_mid, b_mid, w_out, b_out = weights
    col_bf = columns.astype(jnp.bfloat16)
    first = jnp.einsum("ehk,kc->ehc", w_in.astype(jnp.float32), col_bf.astype(jnp.float32)) + b_in[:, :, None]
    first_act = gelu_tanh(first).astype(jnp.bfloat16)
    second = jnp.einsum("ehk,ekc->ehc", w_mid.astype(jnp.float32), first_act.astype(jnp.float32)) + b_mid[:, :, None]
    second_act = gelu_tanh(second).astype(jnp.bfloat16)
    output = jnp.einsum("ezk,ekc->ezc", w_out.astype(jnp.float32), second_act.astype(jnp.float32)) + b_out[:, :, None]
    return col_bf, first, first_act, second, second_act, output


def expert_backward(projected, onehot, saved, weights):
    w_in, b_in, w_mid, b_mid, w_out, b_out = weights
    col_bf, first, first_act, second, second_act = saved
    cot_bf = projected.astype(jnp.bfloat16)
    masked = onehot.astype(jnp.bfloat16)[:, None, :] * cot_bf[None]
    masked_f = masked.astype(jnp.float32)
    d_out = jnp.einsum("ezc,ekc->ezk", masked_f, second_act.astype(jnp.float32))
    db_out = jnp.sum(masked_f, axis=2)
    back_two = jnp.einsum("ezk,ezc->ekc", w_out.astype(jnp.float32), masked_f) * gelu_slope(second)
    back_two_bf = back_two.astype(jnp.bfloat16)
    d_mid = jnp.einsum("ehc,ekc->ehk", back_two_bf.astype(jnp.float32), first_act.astype(jnp.float32))
    db_mid = jnp.sum(back_two, axis=2)
    back_one = jnp.einsum("ehk,ehc->ekc", w_mid.astype(jnp.float32), back_two_bf.astype(jnp.float32)) * gelu_slope(first)
    back_one_bf = back_one.astype(jnp.bfloat16)
    d_in = jnp.einsum("ehc,kc->ehk", back_one_bf.astype(jnp.float32), col_bf.astype(jnp.float32))
    db_in = jnp.sum(back_one, axis=2)
    col_grad = jnp.einsum("ehk,ehc->kc", w_in.astype(jnp.float32), back_one_bf.astype(jnp.float32))
    return col_grad, (d_in, db_in, d_mid, db_mid, d_out, db_out)


def forward_stencil(field, kappa, drift):
    east = jnp.roll(field, -1, axis=1)
    west = jnp.roll(field, 1, axis=1)
    north = jnp.roll(field, -1, axis=2)
    south = jnp.roll(field, 1, axis=2)
    return kappa[None] * (east + west + north + south - 4.0 * field) - drift[:, None, None] * (east - west) * 0.5


def adjoint_stencil(cot, kappa, drift):
    weighted = kappa[None] * cot
    lap = jnp.roll(weighted, -1, axis=1) + jnp.roll(weighted, 1, axis=1) + jnp.roll(weighted, -1, axis=2) + jnp.roll(weighted, 1, axis=2) - 4.0 * weighted
    return lap + drift[:, None, None] * (jnp.roll(cot, -1, axis=1) - jnp.roll(cot, 1, axis=1)) * 0.5


def reference(state, cotangent, kappa, labels, drift, w_in, b_in, w_mid, b_mid, w_out, b_out):
    weights = (w_in, b_in, w_mid, b_mid, w_out, b_out)
    overall = NX * NY
    block = math.gcd(overall, 2048)
    count = overall // block
    regimes = jnp.arange(EXPERTS, dtype=jnp.int32)
    onehot = (labels[None] == regimes[:, None, None]).astype(jnp.float32).reshape(EXPERTS, overall)

    def to_blocks(array):
        return array.reshape(array.shape[0], count, block).transpose(1, 0, 2)

    def from_blocks(array):
        return array.transpose(1, 0, 2).reshape(array.shape[1], overall)

    mask_blocks = to_blocks(onehot)

    def closure(field):
        def one_block(pair):
            saved = expert_forward(pair[0], weights)
            return jnp.sum(pair[1][:, None, :] * saved[5], axis=0)

        mixed = from_blocks(lax.map(one_block, (to_blocks(field.reshape(NZ, overall)), mask_blocks)))
        mixed = mixed - jnp.sum(mixed, axis=1, keepdims=True) / overall
        return mixed.reshape(NZ, NX, NY)

    def closure_back(field, cot):
        projected = cot.reshape(NZ, overall)
        projected = projected - jnp.sum(projected, axis=1, keepdims=True) / overall

        def one_block(carry, item):
            saved = expert_forward(item[0], weights)
            col_grad, grads = expert_backward(item[2], item[1], saved[:5], weights)
            return tuple(a + b for a, b in zip(carry, grads)), col_grad

        start = tuple(jnp.zeros(w.shape, jnp.float32) for w in weights)
        grads, col_blocks = lax.scan(one_block, start, (to_blocks(field.reshape(NZ, overall)), mask_blocks, to_blocks(projected)))
        return from_blocks(col_blocks).reshape(NZ, NX, NY), grads

    section_field = state + step_size * (forward_stencil(state, kappa, drift) + closure(state))
    scaled_late = 0.5 * step_size * cotangent
    late_cols, late_grads = closure_back(section_field, scaled_late)
    mid_grad = 0.5 * cotangent + adjoint_stencil(scaled_late, kappa, drift) + late_cols
    scaled_early = step_size * mid_grad
    early_cols, early_grads = closure_back(state, scaled_early)
    state_grad = 0.5 * cotangent + mid_grad + adjoint_stencil(scaled_early, kappa, drift) + early_cols
    summed = tuple(a + b for a, b in zip(late_grads, early_grads))
    return (state_grad, summed[0], summed[1], summed[2], summed[3], summed[4], summed[5])
```

```python
import functools
import jax
import jax.numpy as jnp
from jax import lax
from jax.experimental import pallas as pl
from jax.experimental.pallas import tpu as pltpu
from jax.sharding import PartitionSpec as P

step_size = 0.8
gelu_coef = 0.7978845608028654
cubic = 0.044715
rows_per_chunk = 4
MESH = pl.DeviceIdType.MESH
f32, bf16 = jnp.float32, jnp.bfloat16


def dot(a, b):
    return jnp.dot(a, b, preferred_element_type=f32)


def dot_nt(a, b):
    return lax.dot_general(a, b, (((1,), (1,)), ((), ())), preferred_element_type=f32)


def gelu_pair(v):
    v2 = v * v
    t = jnp.tanh(v * (gelu_coef + (gelu_coef * cubic) * v2))
    h = 0.5 + 0.5 * t
    z = v * h
    slope = h + z * (1.0 - h) * (2.0 * gelu_coef + (6.0 * gelu_coef * cubic) * v2)
    return z.astype(bf16), slope


def to_row(col, at, nz):
    lane = lax.broadcasted_iota(jnp.int32, (nz, 128), 1)
    sub = lax.broadcasted_iota(jnp.int32, (nz, 128), 0)
    return jnp.sum(jnp.where(lane == sub + at, col, 0.0), axis=0, keepdims=True)


def to_col(row, at, nz):
    lane = lax.broadcasted_iota(jnp.int32, (nz, 128), 1)
    sub = lax.broadcasted_iota(jnp.int32, (nz, 128), 0)
    return jnp.sum(jnp.where(lane == sub + at, row, 0.0), axis=1, keepdims=True)


def main_kernel(
    n, state, cot, kappa, labels, drift, w_in, w_mid, w_out, bias,
    grad_out, sums_out,
    wi, wit, wm, wmt, wot, field, adj, mix, base, z1s, z2s, s1s, s2s, acc, mine, theirs,
    *rest,
):
    levels = rest[: len(rest) - 9]
    (halo_s, halo_r, halo2_s, halo2_r, sum_s, sum_r, red_s, red_r, whole) = rest[len(rest) - 9:]
    nz, nx, ny = state.shape
    ne, hid, _unused = w_in.shape
    nr = rows_per_chunk
    width = nr * ny
    chunks = nx // nr
    overall = nx * ny * n
    me = lax.axis_index("gx")
    right, left = lax.rem(me + 1, n), lax.rem(me + n - 1, n)
    r_in, r_mid, r_out = 0, hid, hid + ne * hid
    r_b = r_out + ne * nz

    barrier = pltpu.get_barrier_semaphore()
    for d in range(1, n):
        pl.semaphore_signal(barrier, inc=1, device_id={"gx": lax.rem(me + d, n)}, device_id_type=MESH)

    late_part = jnp.zeros((nz, ny), f32)
    for i in range(nx):
        c1 = (0.5 * step_size) * cot[:, i, :]
        late_part = late_part + c1
        field[i + 1, 0:nz] = state[:, i, :]
        field[i + 1, nz:2 * nz] = c1
        field[i + 1, 2 * nz:3 * nz] = kappa[i:i + 1, :] * c1
    pl.semaphore_wait(barrier, n - 1)

    def halo(ref, ss, rs):
        a = pltpu.make_async_remote_copy(
            src_ref=ref.at[nx], dst_ref=ref.at[0], send_sem=ss.at[0], recv_sem=rs.at[0],
            device_id={"gx": right}, device_id_type=MESH)
        b = pltpu.make_async_remote_copy(
            src_ref=ref.at[1], dst_ref=ref.at[nx + 1], send_sem=ss.at[1], recv_sem=rs.at[1],
            device_id={"gx": left}, device_id_type=MESH)
        a.start()
        b.start()
        return a, b

    first_halo = halo(field, halo_s, halo_r)

    wi[...] = jnp.concatenate([w_in[e] for e in range(ne)], axis=1)
    wit[...] = wi[...].T
    wm[...] = jnp.concatenate([w_mid[e] for e in range(ne)], axis=1)
    for e in range(ne):
        wmt[:, e * hid:(e + 1) * hid] = w_mid[e].T
    wot[...] = w_out[...].reshape(ne * nz, hid).T
    acc[...] = jnp.zeros_like(acc)

    def lab_of(c):
        return jnp.concatenate([labels[pl.ds(c * nr + r, 1), :] for r in range(nr)], axis=1)

    def pick(lab, parts):
        out = parts[ne - 1]
        for e in range(ne - 2, -1, -1):
            out = jnp.where(lab == e, parts[e], out)
        return out

    def masked(lab, val):
        m = val.shape[0]
        tiled = val.reshape(m // 16, 16, width)
        outs = []
        for e in range(ne):
            oh = jnp.broadcast_to(jnp.where(lab == e, 1.0, 0.0), (16, width)).astype(bf16)
            outs.append((tiled * oh[None]).reshape(m, width))
        return jnp.concatenate(outs, axis=0)

    def bias_of(lab, lo, size):
        return pick(lab, [bias[lo:lo + size, e:e + 1] for e in range(ne)])

    def forward(lab, q):
        hbm = masked(lab, q.astype(bf16))
        z1, s1 = gelu_pair(dot(wi[...], hbm) + bias_of(lab, 0, hid))
        z2, s2 = gelu_pair(dot(wm[...], masked(lab, z1)) + bias_of(lab, hid, hid))
        return hbm, z1, s1, z2, s2

    def add(row, val):
        rows = val.shape[0]
        acc[0, row:row + rows, :] += val[:, 0:128]
        acc[1, row:row + rows, :] += val[:, 128:256]

    def backward(lab, p, hbm, z1, s1, z2, s2):
        hot = jnp.where(lax.broadcasted_iota(jnp.int32, (16, width), 0) == lab, 1.0, 0.0).astype(bf16)
        gy = masked(lab, p.astype(bf16))
        add(r_out, dot_nt(gy, z2))
        add(r_b + 32, dot_nt(jnp.ones((16, width), bf16), gy))
        gab2 = (dot(wot[...], gy) * s2).astype(bf16)
        gab2m = masked(lab, gab2)
        add(r_mid, dot_nt(gab2m, z1))
        add(r_b + 16, dot_nt(hot, gab2))
        gab1 = (dot(wmt[...], gab2m) * s1).astype(bf16)
        add(r_in, dot_nt(gab1, hbm))
        add(r_b, dot_nt(hot, gab1))
        cols = dot(wit[...], gab1)
        return pick(lab, [cols[e * nz:(e + 1) * nz] for e in range(ne)])

    def rowcat(ref, c, lo):
        return jnp.concatenate([ref[c * nr + r + 1, lo:lo + nz] for r in range(nr)], axis=1)

    def first(c, part):
        lab = lab_of(c)
        _, z1, s1, z2, s2 = forward(lab, rowcat(field, c, 0))
        z1s[c], s1s[c], z2s[c], s2s[c] = z1, s1, z2, s2
        y = dot(w_out[...].reshape(ne * nz, hid), z2)
        m = pick(lab, [y[e * nz:(e + 1) * nz] for e in range(ne)]) + bias_of(lab, 2 * hid, nz)
        for r in range(nr):
            block = m[:, r * ny:(r + 1) * ny]
            mix[c * nr + r] = block
            part = part + block
        return part

    mix_part = lax.fori_loop(0, chunks, first, jnp.zeros((nz, ny), f32))

    def exchange(k, row):
        mine[k] = jnp.broadcast_to(row, (8, 128))
        copies = []
        for d in range(1, n):
            copies.append(pltpu.make_async_remote_copy(
                src_ref=mine.at[k], dst_ref=theirs.at[k, d], send_sem=sum_s.at[k, d],
                recv_sem=sum_r.at[k, d], device_id={"gx": lax.rem(me + d, n)}, device_id_type=MESH))
        for copy in copies:
            copy.start()
        return copies

    def collect(k, copies):
        total = mine[k]
        for d in range(1, n):
            copies[d - 1].wait()
            total = total + theirs[k, d]
        return total[0:1] * (1.0 / overall)

    sums = exchange(0, to_row(jnp.sum(mix_part, axis=1, keepdims=True), 0, nz)
                    + to_row(jnp.sum(late_part, axis=1, keepdims=True), nz, nz))
    for copy in first_halo:
        copy.wait()
    means = collect(0, sums)
    mix_mean, late_mean = to_col(means, 0, nz), to_col(means, nz, nz)
    speed = 0.5 * to_col(drift[...], 0, nz)

    def second(c, part):
        lab = lab_of(c)
        qs = []
        for r in range(nr):
            i = c * nr + r
            here, east, west = field[i + 1, 0:nz], field[i + 2, 0:nz], field[i, 0:nz]
            around = east + west + pltpu.roll(here, 127, 1) + pltpu.roll(here, 1, 1) - 4.0 * here
            lq = kappa[pl.ds(i, 1), :] * around - speed * (east - west)
            qs.append(here + step_size * (lq + mix[i] - mix_mean))
        hbm, z1, s1, z2, s2 = forward(lab, jnp.concatenate(qs, axis=1))
        p = rowcat(field, c, nz) - late_mean
        cols = backward(lab, p, hbm, z1, s1, z2, s2)
        for r in range(nr):
            i = c * nr + r
            half_cot = (0.5 / (0.5 * step_size)) * field[i + 1, nz:2 * nz]
            back = adjoint(field, i, nz, 2 * nz) + cols[:, r * ny:(r + 1) * ny]
            mid = half_cot + back
            c0 = step_size * mid
            base[i] = half_cot + mid
            adj[i + 1, 0:nz] = c0
            adj[i + 1, nz:2 * nz] = kappa[pl.ds(i, 1), :] * c0
            part = part + c0
        return part

    def adjoint(ref, i, c_at, k_at):
        k = ref[i + 1, k_at:k_at + nz]
        lap = (ref[i + 2, k_at:k_at + nz] + ref[i, k_at:k_at + nz]
               + pltpu.roll(k, 127, 1) + pltpu.roll(k, 1, 1) - 4.0 * k)
        return lap + speed * (ref[i + 2, c_at:c_at + nz] - ref[i, c_at:c_at + nz])

    early_part = lax.fori_loop(0, chunks, second, jnp.zeros((nz, ny), f32))
    sums = exchange(1, to_row(jnp.sum(early_part, axis=1, keepdims=True), 0, nz))
    second_halo = halo(adj, halo2_s, halo2_r)
    early_mean = to_col(collect(1, sums), 0, nz)
    for copy in second_halo:
        copy.wait()

    def third(c, carry):
        lab = lab_of(c)
        hbm = masked(lab, rowcat(field, c, 0).astype(bf16))
        p = rowcat(adj, c, 0) - early_mean
        cols = backward(lab, p, hbm, z1s[c], s1s[c], z2s[c], s2s[c])
        for r in range(nr):
            i = c * nr + r
            grad_out[i] = base[i] + adjoint(adj, i, 0, nz) + cols[:, r * ny:(r + 1) * ny]
        return carry

    lax.fori_loop(0, chunks, third, 0)

    bits = len(levels)
    orders = [list(range(bits)), [0] + list(range(2, bits)) + [1]]
    total = acc.shape[1]
    offs = [[jnp.int32(0)], [jnp.int32(0)]]

    def plan(s, t):
        b = orders[s][t]
        half = total >> (t + 1)
        bit = lax.rem(me // (1 << b), 2)
        off = offs[s][t]
        keep = pl.multiple_of(off + bit * half, 8)
        send = pl.multiple_of(off + (1 - bit) * half, 8)
        return half, keep, send, me + (1 - 2 * bit) * (1 << b)

    def start_reduce(s, t):
        half, keep, send, partner = plan(s, t)
        copy = pltpu.make_async_remote_copy(
            src_ref=acc.at[s, pl.ds(send, half)], dst_ref=levels[t].at[s], send_sem=red_s.at[s, t],
            recv_sem=red_r.at[s, t], device_id={"gx": partner}, device_id_type=MESH)
        copy.start()
        offs[s].append(keep)
        return copy, half, keep

    def start_gather(s, t):
        half, keep, _, partner = plan(s, t)
        copy = pltpu.make_async_remote_copy(
            src_ref=whole.at[s, pl.ds(keep, half)], dst_ref=whole.at[s, pl.ds(keep, half)],
            send_sem=red_s.at[s, bits + t], recv_sem=red_r.at[s, bits + t],
            device_id={"gx": partner}, device_id_type=MESH)
        copy.start()
        return copy

    flying = [start_reduce(s, 0) for s in range(2)]
    for t in range(bits):
        for s in range(2):
            copy, half, keep = flying[s]
            copy.wait()
            reduced = acc[s, pl.ds(keep, half), :] + levels[t][s]
            if t + 1 < bits:
                acc[s, pl.ds(keep, half), :] = reduced
                flying[s] = start_reduce(s, t + 1)
            else:
                whole[s, pl.ds(keep, half), :] = reduced
                flying[s] = start_gather(s, t)
    for t in range(bits - 1, -1, -1):
        for s in range(2):
            flying[s].wait()
            if t > 0:
                flying[s] = start_gather(s, t - 1)
    sums_out[...] = whole[...]


def output_kernel(grad, sums, state_grad, dw_in, db_in, dw_mid, db_mid, dw_out, db_out):
    ne, hid, nz = dw_in.shape
    r_mid, r_out = hid, hid + ne * hid
    r_b = r_out + ne * nz
    for i in range(grad.shape[0]):
        state_grad[:, i, :] = grad[i]
    per = 128 // nz
    for e in range(ne):
        s, at = e // per, (e % per) * nz
        dw_in[e] = sums[s, 0:hid, at:at + nz]
        db_out[e:e + 1, :] = sums[s, r_b + 32:r_b + 33, at:at + nz]
        for s in range(2):
            lanes = slice(s * 128, (s + 1) * 128)
            dw_mid[e, :, lanes] = sums[s, r_mid + e * hid:r_mid + (e + 1) * hid, :]
            dw_out[e, :, lanes] = sums[s, r_out + e * nz:r_out + (e + 1) * nz, :]
    for s in range(2):
        lanes = slice(s * 128, (s + 1) * 128)
        db_in[:, lanes] = sums[s, r_b:r_b + ne, :]
        db_mid[:, lanes] = sums[s, r_b + 16:r_b + 16 + ne, :]


def shards(state, cotangent, kappa, labels, drift, w_in, b_in, w_mid, b_mid, w_out, b_out):
    nz, nx, ny = state.shape
    ne, hid, _ = w_in.shape
    n = lax.axis_size("gx")
    bits = n.bit_length() - 1
    rows = hid + ne * hid + ne * nz + 8 * n
    bias = jnp.concatenate([b_in, b_mid, b_out], axis=1).T
    drift_row = jnp.pad(drift[None], ((0, 0), (0, 128 - nz)))
    chunks, width = nx // rows_per_chunk, rows_per_chunk * ny
    vmem = pl.BlockSpec(memory_space=pltpu.VMEM)
    sds = jax.ShapeDtypeStruct
    grad, sums = pl.pallas_call(
        functools.partial(main_kernel, n),
        out_shape=(sds((nx, nz, ny), f32), sds((2, rows, 128), f32)),
        in_specs=[vmem] * 9,
        out_specs=(vmem, vmem),
        scratch_shapes=[
            pltpu.VMEM((hid, ne * nz), bf16),
            pltpu.VMEM((ne * nz, hid), bf16),
            pltpu.VMEM((hid, ne * hid), bf16),
            pltpu.VMEM((hid, ne * hid), bf16),
            pltpu.VMEM((hid, ne * nz), bf16),
            pltpu.VMEM((nx + 2, 3 * nz, ny), f32),
            pltpu.VMEM((nx + 2, 2 * nz, ny), f32),
            pltpu.VMEM((nx, nz, ny), f32),
            pltpu.VMEM((nx, nz, ny), f32),
            pltpu.VMEM((chunks, hid, width), bf16),
            pltpu.VMEM((chunks, hid, width), bf16),
            pltpu.VMEM((chunks, hid, width), f32),
            pltpu.VMEM((chunks, hid, width), f32),
            pltpu.VMEM((2, rows, 128), f32),
            pltpu.VMEM((2, 8, 128), f32),
            pltpu.VMEM((2, n, 8, 128), f32),
        ]
        + [pltpu.VMEM((2, rows >> (t + 1), 128), f32) for t in range(bits)]
        + [
            pltpu.SemaphoreType.DMA((2,)),
            pltpu.SemaphoreType.DMA((2,)),
            pltpu.SemaphoreType.DMA((2,)),
            pltpu.SemaphoreType.DMA((2,)),
            pltpu.SemaphoreType.DMA((2, n)),
            pltpu.SemaphoreType.DMA((2, n)),
            pltpu.SemaphoreType.DMA((2, 2 * bits)),
            pltpu.SemaphoreType.DMA((2, 2 * bits)),
            pltpu.VMEM((2, rows, 128), f32),
        ],
        compiler_params=pltpu.CompilerParams(
            collective_id=0, has_side_effects=True, vmem_limit_bytes=48 * 1024 * 1024),
        name="heun_reverse",
    )(state, cotangent, kappa, labels, drift_row, w_in, w_mid, w_out, bias)
    return tuple(pl.pallas_call(
        output_kernel,
        out_shape=(
            sds((nz, nx, ny), f32), sds((ne, hid, nz), f32), sds((ne, hid), f32),
            sds((ne, hid, hid), f32), sds((ne, hid), f32), sds((ne, nz, hid), f32), sds((ne, nz), f32)),
        in_specs=[vmem] * 2,
        out_specs=(vmem,) * 7,
        compiler_params=pltpu.CompilerParams(vmem_limit_bytes=32 * 1024 * 1024),
        name="place_outputs",
    )(grad, sums))


def solution(mesh):
    cells, replicated = P(None, ("parts", "gx"), None), P()
    return jax.shard_map(
        shards,
        mesh=mesh,
        in_specs=(cells, cells, P(("parts", "gx"), None), P(("parts", "gx"), None)) + (replicated,) * 7,
        out_specs=(cells, P("parts", None, None), P("parts", None), P("parts", None, None),
                   P("parts", None), P("parts", None, None), P("parts", None)),
        check_vma=False,
    )
```

```python
import functools
import jax
import jax.numpy as jnp
from jax import lax
from jax.experimental import pallas as pl
from jax.experimental.pallas import tpu as pltpu
from jax.sharding import PartitionSpec as P

step_size = 0.8
gelu_coef = 0.7978845608028654
cubic = 0.044715
rows_per_chunk = 16
MESH = pl.DeviceIdType.MESH
f32, bf16 = jnp.float32, jnp.bfloat16


def dot(a, b):
    return jnp.dot(a, b, preferred_element_type=f32)


def dot_nt(a, b):
    return lax.dot_general(a, b, (((1,), (1,)), ((), ())), preferred_element_type=f32)


def gelu_pair(v):
    v2 = v * v
    t = jnp.tanh(v * (gelu_coef + (gelu_coef * cubic) * v2))
    h = 0.5 + 0.5 * t
    z = v * h
    slope = h + z * (1.0 - h) * (2.0 * gelu_coef + (6.0 * gelu_coef * cubic) * v2)
    return z.astype(bf16), slope


def to_row(col, at, nz):
    lane = lax.broadcasted_iota(jnp.int32, (nz, 128), 1)
    sub = lax.broadcasted_iota(jnp.int32, (nz, 128), 0)
    return jnp.sum(jnp.where(lane == sub + at, col, 0.0), axis=0, keepdims=True)


def to_col(row, at, nz):
    shape = (nz, row.shape[1])
    lane = lax.broadcasted_iota(jnp.int32, shape, 1)
    sub = lax.broadcasted_iota(jnp.int32, shape, 0)
    return jnp.sum(jnp.where(lane == sub + at, row, 0.0), axis=1, keepdims=True)


def main_kernel(
    n, state_h, cot_h, kappa_h, labels_h, drift_h, w_in_h, w_mid_h, w_out_h, b_in_h, b_mid_h, b_out_h,
    grad_out, sums_out,
    state, cot, kappa, labels, drift, w_in, w_mid, w_out, b_in, b_mid, b_out, load, bias,
    wi, wit, wm, wmt, wot, field, adj, mix, base, z1s, z2s, s1s, s2s, acc, mine, theirs,
    inbox, halo_s, halo_r, halo2_s, halo2_r, sum_s, sum_r, red_s, red_r, whole,
):
    nz, nx, ny = state.shape
    ne, nz_in, hid = w_in.shape
    nr = rows_per_chunk
    width = nr * ny
    chunks = nx // nr
    overall = nx * ny * n
    me = lax.axis_index("gx")
    right, left = lax.rem(me + 1, n), lax.rem(me + n - 1, n)
    r_in, r_mid, r_out = 0, ne * nz, ne * nz + ne * hid
    r_b = r_out + ne * nz

    barrier = pltpu.get_barrier_semaphore()
    for d in range(1, n):
        pl.semaphore_signal(barrier, inc=1, device_id={"gx": lax.rem(me + d, n)}, device_id_type=MESH)

    pairs = [(state_h, state), (cot_h, cot), (kappa_h, kappa), (labels_h, labels), (drift_h, drift),
             (w_in_h, w_in), (w_mid_h, w_mid), (w_out_h, w_out), (b_in_h, b_in), (b_mid_h, b_mid),
             (b_out_h, b_out)]
    loads = [pltpu.make_async_copy(src, dst, load.at[i]) for i, (src, dst) in enumerate(pairs)]
    for i in (0, 1, 2, 5, 6, 7, 8, 9, 10, 3, 4):
        loads[i].start()
    for i in (0, 1, 2):
        loads[i].wait()
    late_part = jnp.zeros((nz, ny), f32)
    for i in range(nx):
        c1 = (0.5 * step_size) * cot[:, i, :]
        late_part = late_part + c1
        field[i + 1, 0:nz] = state[:, i, :]
        field[i + 1, nz:2 * nz] = c1
        field[i + 1, 2 * nz:3 * nz] = kappa[i:i + 1, :] * c1
    pl.semaphore_wait(barrier, n - 1)

    def halo(ref, ss, rs):
        a = pltpu.make_async_remote_copy(
            src_ref=ref.at[nx], dst_ref=ref.at[0], send_sem=ss.at[0], recv_sem=rs.at[0],
            device_id={"gx": right}, device_id_type=MESH)
        b = pltpu.make_async_remote_copy(
            src_ref=ref.at[1], dst_ref=ref.at[nx + 1], send_sem=ss.at[1], recv_sem=rs.at[1],
            device_id={"gx": left}, device_id_type=MESH)
        a.start()
        b.start()
        return a, b

    first_halo = halo(field, halo_s, halo_r)

    for i in range(3, len(loads)):
        loads[i].wait()
    wit[...] = w_in[...].reshape(ne * nz, hid)
    wi[...] = wit[...].T
    at = 0
    for b in (b_in, b_mid, b_out):
        size = b.shape[1]
        bias[at:at + size] = jnp.concatenate([b[...], jnp.zeros((8 - ne, size), f32)], axis=0).T
        at += size
    wm[...] = jnp.concatenate([w_mid[e] for e in range(ne)], axis=1)
    for e in range(ne):
        wmt[:, e * hid:(e + 1) * hid] = w_mid[e].T
    wot[...] = w_out[...].reshape(ne * nz, hid).T
    acc[...] = jnp.zeros_like(acc)

    def lab_of(c):
        return jnp.concatenate([labels[pl.ds(c * nr + r, 1), :] for r in range(nr)], axis=1)

    def pick(lab, parts):
        out = parts[ne - 1]
        for e in range(ne - 2, -1, -1):
            out = jnp.where(lab == e, parts[e], out)
        return out

    def masked(lab, val):
        m = val.shape[0]
        tiled = val.reshape(m // 16, 16, width)
        outs = []
        for e in range(ne):
            oh = jnp.broadcast_to(jnp.where(lab == e, 1.0, 0.0), (16, width)).astype(bf16)
            outs.append((tiled * oh[None]).reshape(m, width))
        return jnp.concatenate(outs, axis=0)

    def bias_of(lab, lo, size):
        return pick(lab, [bias[lo:lo + size, e:e + 1] for e in range(ne)])

    def forward(lab, q):
        hbm = masked(lab, q.astype(bf16))
        z1, s1 = gelu_pair(dot(wi[...], hbm) + bias_of(lab, 0, hid))
        z2, s2 = gelu_pair(dot(wm[...], masked(lab, z1)) + bias_of(lab, hid, hid))
        return hbm, z1, s1, z2, s2

    def add(row, val):
        rows = val.shape[0]
        acc[0, row:row + rows, :] += val[:, 0:128]
        acc[1, row:row + rows, :] += val[:, 128:256]

    def backward(lab, p, hbm, z1, s1, z2, s2):
        hot = jnp.where(lax.broadcasted_iota(jnp.int32, (16, width), 0) == lab, 1.0, 0.0).astype(bf16)
        gy = masked(lab, p.astype(bf16))
        add(r_out, dot_nt(gy, z2))
        add(r_b + 32, dot_nt(jnp.ones((16, width), bf16), gy))
        gab2 = (dot(wot[...], gy) * s2).astype(bf16)
        gab2m = masked(lab, gab2)
        add(r_mid, dot_nt(gab2m, z1))
        add(r_b + 16, dot_nt(hot, gab2))
        gab1 = (dot(wmt[...], gab2m) * s1).astype(bf16)
        add(r_in, dot_nt(hbm, gab1))
        add(r_b, dot_nt(hot, gab1))
        cols = dot(wit[...], gab1)
        return pick(lab, [cols[e * nz:(e + 1) * nz] for e in range(ne)])

    def rowcat(ref, c, lo):
        return jnp.concatenate([ref[c * nr + r + 1, lo:lo + nz] for r in range(nr)], axis=1)

    def first(c, part):
        lab = lab_of(c)
        _, z1, s1, z2, s2 = forward(lab, rowcat(field, c, 0))
        z1s[c], s1s[c], z2s[c], s2s[c] = z1, s1, z2, s2
        y = dot(w_out[...].reshape(ne * nz, hid), z2)
        m = pick(lab, [y[e * nz:(e + 1) * nz] for e in range(ne)]) + bias_of(lab, 2 * hid, nz)
        for r in range(nr):
            block = m[:, r * ny:(r + 1) * ny]
            mix[c * nr + r] = block
            part = part + block
        return part

    mix_part = lax.fori_loop(0, chunks, first, jnp.zeros((nz, ny), f32))

    def exchange(k, row):
        mine[k] = jnp.broadcast_to(row, (8, 128))
        copies = []
        for d in range(1, n):
            copies.append(pltpu.make_async_remote_copy(
                src_ref=mine.at[k], dst_ref=theirs.at[k, d], send_sem=sum_s.at[k, d],
                recv_sem=sum_r.at[k, d], device_id={"gx": lax.rem(me + d, n)}, device_id_type=MESH))
        for copy in copies:
            copy.start()
        return copies

    def collect(k, copies):
        total = mine[k]
        for d in range(1, n):
            copies[d - 1].wait()
            total = total + theirs[k, d]
        return total[0:1] * (1.0 / overall)

    sums = exchange(0, to_row(jnp.sum(mix_part, axis=1, keepdims=True), 0, nz)
                    + to_row(jnp.sum(late_part, axis=1, keepdims=True), nz, nz))
    for copy in first_halo:
        copy.wait()
    means = collect(0, sums)
    mix_mean, late_mean = to_col(means, 0, nz), to_col(means, nz, nz)
    speed = 0.5 * to_col(drift[...], 0, nz)

    def second(c, part):
        lab = lab_of(c)
        qs = []
        for r in range(nr):
            i = c * nr + r
            here, east, west = field[i + 1, 0:nz], field[i + 2, 0:nz], field[i, 0:nz]
            around = east + west + pltpu.roll(here, 127, 1) + pltpu.roll(here, 1, 1) - 4.0 * here
            lq = kappa[pl.ds(i, 1), :] * around - speed * (east - west)
            qs.append(here + step_size * (lq + mix[i] - mix_mean))
        hbm, z1, s1, z2, s2 = forward(lab, jnp.concatenate(qs, axis=1))
        p = rowcat(field, c, nz) - late_mean
        cols = backward(lab, p, hbm, z1, s1, z2, s2)
        for r in range(nr):
            i = c * nr + r
            half_cot = (0.5 / (0.5 * step_size)) * field[i + 1, nz:2 * nz]
            back = adjoint(field, i, nz, 2 * nz) + cols[:, r * ny:(r + 1) * ny]
            mid = half_cot + back
            c0 = step_size * mid
            base[i] = half_cot + mid
            adj[i + 1, 0:nz] = c0
            adj[i + 1, nz:2 * nz] = kappa[pl.ds(i, 1), :] * c0
            part = part + c0
        return part

    def adjoint(ref, i, c_at, k_at):
        k = ref[i + 1, k_at:k_at + nz]
        lap = (ref[i + 2, k_at:k_at + nz] + ref[i, k_at:k_at + nz]
               + pltpu.roll(k, 127, 1) + pltpu.roll(k, 1, 1) - 4.0 * k)
        return lap + speed * (ref[i + 2, c_at:c_at + nz] - ref[i, c_at:c_at + nz])

    early_part = lax.fori_loop(0, chunks, second, jnp.zeros((nz, ny), f32))
    sums = exchange(1, to_row(jnp.sum(early_part, axis=1, keepdims=True), 0, nz))
    second_halo = halo(adj, halo2_s, halo2_r)
    early_mean = to_col(collect(1, sums), 0, nz)
    for copy in second_halo:
        copy.wait()

    def third(c, carry):
        lab = lab_of(c)
        hbm = masked(lab, rowcat(field, c, 0).astype(bf16))
        p = rowcat(adj, c, 0) - early_mean
        cols = backward(lab, p, hbm, z1s[c], s1s[c], z2s[c], s2s[c])
        for r in range(nr):
            i = c * nr + r
            grad_out[i] = base[i] + adjoint(adj, i, 0, nz) + cols[:, r * ny:(r + 1) * ny]
        return carry

    lax.fori_loop(0, chunks, third, 0)

    bits = n.bit_length() - 1
    units = acc.shape[1] // (8 * n)
    low = (units // 2) * 8 * n
    rest_bits = [list(range(b, b + 1)) for b in range(2, bits)]
    near_first = [[0], [1]] + rest_bits
    far_first = [[0]] + rest_bits + [[1]]
    streams = [(0, 0, low, near_first), (1, 0, low, far_first),
               (0, low, acc.shape[1] - low, far_first), (1, low, acc.shape[1] - low, near_first)]
    stages = len(near_first)
    digit = [lax.rem(me // (1 << b), 2) for b in range(bits)]
    states = [[(jnp.int32(row), size, row)] for _, row, size, _ in streams]

    def plan(s, t):
        lanes, _, _, order = streams[s]
        off, size, slot = states[s][t]
        group = order[t]
        part = size >> len(group)
        peers = []
        for m in range(1 << len(group)):
            place, device = 0, me
            for j, b in enumerate(group):
                flip = (m >> j) & 1
                place = place + (1 - digit[b] if flip else digit[b]) * (1 << j)
                device = device + flip * (1 - 2 * digit[b]) * (1 << b)
            peers.append((pl.multiple_of(off + place * part, 8), device))
        return lanes, part, slot, peers

    def start_reduce(s, t):
        lanes, part, slot, peers = plan(s, t)
        copies = []
        for m in range(1, len(peers)):
            region, device = peers[m]
            copy = pltpu.make_async_remote_copy(
                src_ref=acc.at[lanes, pl.ds(region, part)],
                dst_ref=inbox.at[lanes, pl.ds(slot + (m - 1) * part, part)],
                send_sem=red_s.at[s, t, m - 1], recv_sem=red_r.at[s, t, m - 1],
                device_id={"gx": device}, device_id_type=MESH)
            copy.start()
            copies.append(copy)
        states[s].append((peers[0][0], part, slot + (len(peers) - 1) * part))
        return copies

    def start_gather(s, t):
        lanes, part, _, peers = plan(s, t)
        kept = whole.at[lanes, pl.ds(peers[0][0], part)]
        copies = []
        for m in range(1, len(peers)):
            copy = pltpu.make_async_remote_copy(
                src_ref=kept, dst_ref=kept,
                send_sem=red_s.at[s, stages + t, m - 1], recv_sem=red_r.at[s, stages + t, m - 1],
                device_id={"gx": peers[m][1]}, device_id_type=MESH)
            copy.start()
            copies.append(copy)
        return copies

    flying = [start_reduce(s, 0) for s in range(len(streams))]
    for t in range(stages):
        for s in range(len(streams)):
            lanes, part, slot, peers = plan(s, t)
            for copy in flying[s]:
                copy.wait()
            reduced = acc[lanes, pl.ds(peers[0][0], part), :]
            for m in range(len(peers) - 1):
                reduced = reduced + inbox[lanes, slot + m * part:slot + (m + 1) * part, :]
            if t + 1 < stages:
                acc[lanes, pl.ds(peers[0][0], part), :] = reduced
                flying[s] = start_reduce(s, t + 1)
            else:
                whole[lanes, pl.ds(peers[0][0], part), :] = reduced
                flying[s] = start_gather(s, t)
    for t in range(stages - 1, -1, -1):
        for s in range(len(streams)):
            for copy in flying[s]:
                copy.wait()
            if t > 0:
                flying[s] = start_gather(s, t - 1)
    sums_out[...] = whole[...]


def output_kernel(grad, sums, state_grad, dw_in, db_in, dw_mid, db_mid, dw_out, db_out):
    ne, nz, hid = dw_in.shape
    r_mid, r_out = ne * nz, ne * nz + ne * hid
    r_b = r_out + ne * nz
    for i in range(grad.shape[0]):
        state_grad[:, i, :] = grad[i]
    per = 128 // nz
    for e in range(ne):
        s, at = e // per, (e % per) * nz
        db_out[e:e + 1, :] = sums[s, r_b + 32:r_b + 33, at:at + nz]
        for s in range(2):
            lanes = slice(s * 128, (s + 1) * 128)
            dw_in[e, :, lanes] = sums[s, e * nz:(e + 1) * nz, :]
            dw_mid[e, :, lanes] = sums[s, r_mid + e * hid:r_mid + (e + 1) * hid, :]
            dw_out[e, :, lanes] = sums[s, r_out + e * nz:r_out + (e + 1) * nz, :]
    for s in range(2):
        lanes = slice(s * 128, (s + 1) * 128)
        db_in[:, lanes] = sums[s, r_b:r_b + ne, :]
        db_mid[:, lanes] = sums[s, r_b + 16:r_b + 16 + ne, :]


def shards(state, cotangent, kappa, labels, drift, w_in, b_in, w_mid, b_mid, w_out, b_out):
    nz, nx, ny = state.shape
    ne, hid, _ = w_in.shape
    n = lax.axis_size("gx")
    bits = n.bit_length() - 1
    rows = ne * nz + ne * hid + ne * nz + 8 * n
    operands = (state, cotangent, kappa, labels, drift[None], jnp.transpose(w_in, (0, 2, 1)), w_mid, w_out,
                b_in, b_mid, b_out)
    chunks, width = nx // rows_per_chunk, rows_per_chunk * ny
    vmem = pl.BlockSpec(memory_space=pltpu.VMEM)
    sds = jax.ShapeDtypeStruct
    grad, sums = pl.pallas_call(
        functools.partial(main_kernel, n),
        out_shape=(sds((nx, nz, ny), f32), sds((2, rows, 128), f32)),
        in_specs=[pl.BlockSpec(memory_space=pltpu.HBM)] * len(operands),
        out_specs=(vmem, vmem),
        scratch_shapes=[pltpu.VMEM(x.shape, x.dtype) for x in operands]
        + [
            pltpu.SemaphoreType.DMA((len(operands),)),
            pltpu.VMEM((2 * hid + nz, 8), f32),
            pltpu.VMEM((hid, ne * nz), bf16),
            pltpu.VMEM((ne * nz, hid), bf16),
            pltpu.VMEM((hid, ne * hid), bf16),
            pltpu.VMEM((hid, ne * hid), bf16),
            pltpu.VMEM((hid, ne * nz), bf16),
            pltpu.VMEM((nx + 2, 3 * nz, ny), f32),
            pltpu.VMEM((nx + 2, 2 * nz, ny), f32),
            pltpu.VMEM((nx, nz, ny), f32),
            pltpu.VMEM((nx, nz, ny), f32),
            pltpu.VMEM((chunks, hid, width), bf16),
            pltpu.VMEM((chunks, hid, width), bf16),
            pltpu.VMEM((chunks, hid, width), f32),
            pltpu.VMEM((chunks, hid, width), f32),
            pltpu.VMEM((2, rows, 128), f32),
            pltpu.VMEM((2, 8, 128), f32),
            pltpu.VMEM((2, n, 8, 128), f32),
        ]
        + [
            pltpu.VMEM((2, rows, 128), f32),
            pltpu.SemaphoreType.DMA((2,)),
            pltpu.SemaphoreType.DMA((2,)),
            pltpu.SemaphoreType.DMA((2,)),
            pltpu.SemaphoreType.DMA((2,)),
            pltpu.SemaphoreType.DMA((2, n)),
            pltpu.SemaphoreType.DMA((2, n)),
            pltpu.SemaphoreType.DMA((4, 2 * bits, 3)),
            pltpu.SemaphoreType.DMA((4, 2 * bits, 3)),
            pltpu.VMEM((2, rows, 128), f32),
        ],
        compiler_params=pltpu.CompilerParams(
            collective_id=0, has_side_effects=True, vmem_limit_bytes=62 * 1024 * 1024),
        name="heun_reverse",
    )(*operands)
    outs = pl.pallas_call(
        output_kernel,
        out_shape=(
            sds((nz, nx, ny), f32), sds((ne, nz, hid), f32), sds((ne, hid), f32),
            sds((ne, hid, hid), f32), sds((ne, hid), f32), sds((ne, nz, hid), f32), sds((ne, nz), f32)),
        in_specs=[vmem] * 2,
        out_specs=(vmem,) * 7,
        compiler_params=pltpu.CompilerParams(vmem_limit_bytes=32 * 1024 * 1024),
        name="place_outputs",
    )(grad, sums)
    return (outs[0], jnp.transpose(outs[1], (0, 2, 1))) + tuple(outs[2:])


def solution(mesh):
    cells, replicated = P(None, ("parts", "gx"), None), P()
    return jax.shard_map(
        shards,
        mesh=mesh,
        in_specs=(cells, cells, P(("parts", "gx"), None), P(("parts", "gx"), None)) + (replicated,) * 7,
        out_specs=(cells, P("parts", None, None), P("parts", None), P("parts", None, None),
                   P("parts", None), P("parts", None, None), P("parts", None)),
        check_vma=False,
    )
```

```python
import functools
import jax
import jax.numpy as jnp
from jax import lax
from jax.experimental import pallas as pl
from jax.experimental.pallas import tpu as pltpu
from jax.sharding import PartitionSpec as P

step_size = 0.8
gelu_coef = 0.7978845608028654
cubic = 0.044715
rows_per_chunk = 16
MESH = pl.DeviceIdType.MESH
f32, bf16 = jnp.float32, jnp.bfloat16


def dot(a, b):
    return jnp.dot(a, b, preferred_element_type=f32)


def dot_nt(a, b):
    return lax.dot_general(a, b, (((1,), (1,)), ((), ())), preferred_element_type=f32)


def gelu_pair(v):
    v2 = v * v
    t = jnp.tanh(v * (gelu_coef + (gelu_coef * cubic) * v2))
    h = 0.5 + 0.5 * t
    z = v * h
    slope = h + z * (1.0 - h) * (2.0 * gelu_coef + (6.0 * gelu_coef * cubic) * v2)
    return z.astype(bf16), slope


def to_row(col, at, nz):
    lane = lax.broadcasted_iota(jnp.int32, (nz, 128), 1)
    sub = lax.broadcasted_iota(jnp.int32, (nz, 128), 0)
    return jnp.sum(jnp.where(lane == sub + at, col, 0.0), axis=0, keepdims=True)


def to_col(row, at, nz):
    shape = (nz, row.shape[1])
    lane = lax.broadcasted_iota(jnp.int32, shape, 1)
    sub = lax.broadcasted_iota(jnp.int32, shape, 0)
    return jnp.sum(jnp.where(lane == sub + at, row, 0.0), axis=1, keepdims=True)


def main_kernel(
    n, state_h, cot_h, kappa_h, labels_h, drift_h, w_in_h, w_mid_h, w_out_h, b_in_h, b_mid_h, b_out_h,
    grad_out, sums_out,
    state, cot, kappa, labels, drift, w_in, w_mid, w_out, b_in, b_mid, b_out, load, bias,
    wi, wit, wm, wmt, wot, field, adj, mix, base, z1s, z2s, s1s, s2s, acc, mine, theirs,
    inbox, halo_s, halo_r, halo2_s, halo2_r, sum_s, sum_r, red_s, red_r, whole,
):
    nz, nx, ny = state.shape
    ne, nz_in, hid = w_in.shape
    nr = rows_per_chunk
    width = nr * ny
    chunks = nx // nr
    overall = nx * ny * n
    me = lax.axis_index("gx")
    right, left = lax.rem(me + 1, n), lax.rem(me + n - 1, n)
    r_in, r_mid, r_out = 0, ne * nz + 16, ne * nz + 16 + ne * hid
    r_b = r_out + ne * nz

    barrier = pltpu.get_barrier_semaphore()
    for d in range(1, n):
        pl.semaphore_signal(barrier, inc=1, device_id={"gx": lax.rem(me + d, n)}, device_id_type=MESH)

    pairs = [(state_h, state), (cot_h, cot), (kappa_h, kappa), (labels_h, labels), (drift_h, drift),
             (w_in_h, w_in), (w_mid_h, w_mid), (w_out_h, w_out), (b_in_h, b_in), (b_mid_h, b_mid),
             (b_out_h, b_out)]
    loads = [pltpu.make_async_copy(src, dst, load.at[i]) for i, (src, dst) in enumerate(pairs)]
    for i in (0, 1, 2, 5, 6, 7, 8, 9, 10, 3, 4):
        loads[i].start()
    for i in (0, 1, 2):
        loads[i].wait()
    late_part = jnp.zeros((nz, ny), f32)
    for i in range(nx):
        c1 = (0.5 * step_size) * cot[:, i, :]
        late_part = late_part + c1
        field[i + 1, 0:nz] = state[:, i, :]
        field[i + 1, nz:2 * nz] = c1
        field[i + 1, 2 * nz:3 * nz] = kappa[i:i + 1, :] * c1
    pl.semaphore_wait(barrier, n - 1)

    def halo(ref, ss, rs):
        a = pltpu.make_async_remote_copy(
            src_ref=ref.at[nx], dst_ref=ref.at[0], send_sem=ss.at[0], recv_sem=rs.at[0],
            device_id={"gx": right}, device_id_type=MESH)
        b = pltpu.make_async_remote_copy(
            src_ref=ref.at[1], dst_ref=ref.at[nx + 1], send_sem=ss.at[1], recv_sem=rs.at[1],
            device_id={"gx": left}, device_id_type=MESH)
        a.start()
        b.start()
        return a, b

    first_halo = halo(field, halo_s, halo_r)

    for i in range(3, len(loads)):
        loads[i].wait()
    wit[...] = w_in[...].reshape(ne * nz, hid)
    wi[...] = wit[...].T
    at = 0
    for b in (b_in, b_mid, b_out):
        size = b.shape[1]
        bias[at:at + size] = jnp.concatenate([b[...], jnp.zeros((8 - ne, size), f32)], axis=0).T
        at += size
    wm[...] = jnp.concatenate([w_mid[e] for e in range(ne)], axis=1)
    for e in range(ne):
        wmt[:, e * hid:(e + 1) * hid] = w_mid[e].T
    wot[...] = w_out[...].reshape(ne * nz, hid).T
    acc[...] = jnp.zeros_like(acc)

    def lab_of(c):
        return jnp.concatenate([labels[pl.ds(c * nr + r, 1), :] for r in range(nr)], axis=1)

    def pick(lab, parts):
        out = parts[ne - 1]
        for e in range(ne - 2, -1, -1):
            out = jnp.where(lab == e, parts[e], out)
        return out

    def masked(lab, val):
        m = val.shape[0]
        tiled = val.reshape(m // 16, 16, width)
        outs = []
        for e in range(ne):
            oh = jnp.broadcast_to(jnp.where(lab == e, 1.0, 0.0), (16, width)).astype(bf16)
            outs.append((tiled * oh[None]).reshape(m, width))
        return jnp.concatenate(outs, axis=0)

    def bias_of(lab, lo, size):
        return pick(lab, [bias[lo:lo + size, e:e + 1] for e in range(ne)])

    def forward(lab, q):
        hbm = masked(lab, q.astype(bf16))
        z1, s1 = gelu_pair(dot(wi[...], hbm) + bias_of(lab, 0, hid))
        z2, s2 = gelu_pair(dot(wm[...], masked(lab, z1)) + bias_of(lab, hid, hid))
        return hbm, z1, s1, z2, s2

    def add(row, val):
        rows = val.shape[0]
        acc[0, row:row + rows, :] += val[:, 0:128]
        acc[1, row:row + rows, :] += val[:, 128:256]

    def backward(lab, p, hbm, z1, s1, z2, s2, ready=None):
        hot = jnp.where(lax.broadcasted_iota(jnp.int32, (16, width), 0) == lab, 1.0, 0.0).astype(bf16)
        gy = masked(lab, p.astype(bf16))
        add(r_out, dot_nt(gy, z2))
        add(r_b + 32, dot_nt(jnp.ones((16, width), bf16), gy))
        gab2 = (dot(wot[...], gy) * s2).astype(bf16)
        gab2m = masked(lab, gab2)
        add(r_mid, dot_nt(gab2m, z1))
        add(r_b + 16, dot_nt(hot, gab2))
        if ready is not None:
            ready()
        gab1 = (dot(wmt[...], gab2m) * s1).astype(bf16)
        add(r_in, dot_nt(hbm, gab1))
        add(ne * nz, dot_nt(hot, gab1))
        cols = dot(wit[...], gab1)
        return pick(lab, [cols[e * nz:(e + 1) * nz] for e in range(ne)])

    def rowcat(ref, c, lo):
        return jnp.concatenate([ref[c * nr + r + 1, lo:lo + nz] for r in range(nr)], axis=1)

    def first(c, part):
        lab = lab_of(c)
        _, z1, s1, z2, s2 = forward(lab, rowcat(field, c, 0))
        z1s[c], s1s[c], z2s[c], s2s[c] = z1, s1, z2, s2
        y = dot(w_out[...].reshape(ne * nz, hid), z2)
        m = pick(lab, [y[e * nz:(e + 1) * nz] for e in range(ne)]) + bias_of(lab, 2 * hid, nz)
        for r in range(nr):
            block = m[:, r * ny:(r + 1) * ny]
            mix[c * nr + r] = block
            part = part + block
        return part

    mix_part = lax.fori_loop(0, chunks, first, jnp.zeros((nz, ny), f32))

    def exchange(k, row):
        mine[k] = jnp.broadcast_to(row, (8, 128))
        copies = []
        for d in range(1, n):
            copies.append(pltpu.make_async_remote_copy(
                src_ref=mine.at[k], dst_ref=theirs.at[k, d], send_sem=sum_s.at[k, d],
                recv_sem=sum_r.at[k, d], device_id={"gx": lax.rem(me + d, n)}, device_id_type=MESH))
        for copy in copies:
            copy.start()
        return copies

    def collect(k, copies):
        total = mine[k]
        for d in range(1, n):
            copies[d - 1].wait()
            total = total + theirs[k, d]
        return total[0:1] * (1.0 / overall)

    sums = exchange(0, to_row(jnp.sum(mix_part, axis=1, keepdims=True), 0, nz)
                    + to_row(jnp.sum(late_part, axis=1, keepdims=True), nz, nz))
    for copy in first_halo:
        copy.wait()
    means = collect(0, sums)
    mix_mean, late_mean = to_col(means, 0, nz), to_col(means, nz, nz)
    speed = 0.5 * to_col(drift[...], 0, nz)

    def second(c, part):
        lab = lab_of(c)
        qs = []
        for r in range(nr):
            i = c * nr + r
            here, east, west = field[i + 1, 0:nz], field[i + 2, 0:nz], field[i, 0:nz]
            around = east + west + pltpu.roll(here, 127, 1) + pltpu.roll(here, 1, 1) - 4.0 * here
            lq = kappa[pl.ds(i, 1), :] * around - speed * (east - west)
            qs.append(here + step_size * (lq + mix[i] - mix_mean))
        hbm, z1, s1, z2, s2 = forward(lab, jnp.concatenate(qs, axis=1))
        p = rowcat(field, c, nz) - late_mean
        cols = backward(lab, p, hbm, z1, s1, z2, s2)
        for r in range(nr):
            i = c * nr + r
            half_cot = (0.5 / (0.5 * step_size)) * field[i + 1, nz:2 * nz]
            back = adjoint(field, i, nz, 2 * nz) + cols[:, r * ny:(r + 1) * ny]
            mid = half_cot + back
            c0 = step_size * mid
            base[i] = half_cot + mid
            adj[i + 1, 0:nz] = c0
            adj[i + 1, nz:2 * nz] = kappa[pl.ds(i, 1), :] * c0
            part = part + c0
        return part

    def adjoint(ref, i, c_at, k_at):
        k = ref[i + 1, k_at:k_at + nz]
        lap = (ref[i + 2, k_at:k_at + nz] + ref[i, k_at:k_at + nz]
               + pltpu.roll(k, 127, 1) + pltpu.roll(k, 1, 1) - 4.0 * k)
        return lap + speed * (ref[i + 2, c_at:c_at + nz] - ref[i, c_at:c_at + nz])

    early_part = lax.fori_loop(0, chunks, second, jnp.zeros((nz, ny), f32))
    sums = exchange(1, to_row(jnp.sum(early_part, axis=1, keepdims=True), 0, nz))
    second_halo = halo(adj, halo2_s, halo2_r)
    early_mean = to_col(collect(1, sums), 0, nz)
    for copy in second_halo:
        copy.wait()

    def third(c, ready=None):
        lab = lab_of(c)
        hbm = masked(lab, rowcat(field, c, 0).astype(bf16))
        p = rowcat(adj, c, 0) - early_mean
        cols = backward(lab, p, hbm, z1s[c], s1s[c], z2s[c], s2s[c], ready)
        for r in range(nr):
            i = c * nr + r
            grad_out[i] = base[i] + adjoint(adj, i, 0, nz) + cols[:, r * ny:(r + 1) * ny]

    bits = n.bit_length() - 1
    units = acc.shape[1] // (8 * n)
    low = (units // 2) * 8 * n
    rest_bits = [list(range(b, b + 1)) for b in range(2, bits)]
    near_first = [[0], [1]] + rest_bits
    far_first = [[0]] + rest_bits + [[1]]
    streams = [(0, 0, low, near_first), (1, 0, low, far_first),
               (0, low, acc.shape[1] - low, far_first), (1, low, acc.shape[1] - low, near_first)]
    stages = len(near_first)
    digit = [lax.rem(me // (1 << b), 2) for b in range(bits)]
    states = [[(jnp.int32(row), size, row)] for _, row, size, _ in streams]

    def plan(s, t):
        lanes, _, _, order = streams[s]
        off, size, slot = states[s][t]
        group = order[t]
        part = size >> len(group)
        peers = []
        for m in range(1 << len(group)):
            place, device = 0, me
            for j, b in enumerate(group):
                flip = (m >> j) & 1
                place = place + (1 - digit[b] if flip else digit[b]) * (1 << j)
                device = device + flip * (1 - 2 * digit[b]) * (1 << b)
            peers.append((pl.multiple_of(off + place * part, 8), device))
        return lanes, part, slot, peers

    def start_reduce(s, t):
        lanes, part, slot, peers = plan(s, t)
        copies = []
        for m in range(1, len(peers)):
            region, device = peers[m]
            copy = pltpu.make_async_remote_copy(
                src_ref=acc.at[lanes, pl.ds(region, part)],
                dst_ref=inbox.at[lanes, pl.ds(slot + (m - 1) * part, part)],
                send_sem=red_s.at[s, t, m - 1], recv_sem=red_r.at[s, t, m - 1],
                device_id={"gx": device}, device_id_type=MESH)
            copy.start()
            copies.append(copy)
        states[s].append((peers[0][0], part, slot + (len(peers) - 1) * part))
        return copies

    def start_gather(s, t):
        lanes, part, _, peers = plan(s, t)
        kept = whole.at[lanes, pl.ds(peers[0][0], part)]
        copies = []
        for m in range(1, len(peers)):
            copy = pltpu.make_async_remote_copy(
                src_ref=kept, dst_ref=kept,
                send_sem=red_s.at[s, stages + t, m - 1], recv_sem=red_r.at[s, stages + t, m - 1],
                device_id={"gx": peers[m][1]}, device_id_type=MESH)
            copy.start()
            copies.append(copy)
        return copies

    flying = {}

    def begin_high():
        for s in (2, 3):
            flying[s] = start_reduce(s, 0)

    early_start = low >= ne * nz + 16
    for c in range(chunks):
        third(c, begin_high if early_start and c == chunks - 1 else None)
    if not early_start:
        begin_high()
    for s in (0, 1):
        flying[s] = start_reduce(s, 0)
    for t in range(stages):
        for s in (2, 3, 0, 1):
            lanes, part, slot, peers = plan(s, t)
            for copy in flying[s]:
                copy.wait()
            reduced = acc[lanes, pl.ds(peers[0][0], part), :]
            for m in range(len(peers) - 1):
                reduced = reduced + inbox[lanes, slot + m * part:slot + (m + 1) * part, :]
            if t + 1 < stages:
                acc[lanes, pl.ds(peers[0][0], part), :] = reduced
                flying[s] = start_reduce(s, t + 1)
            else:
                whole[lanes, pl.ds(peers[0][0], part), :] = reduced
                flying[s] = start_gather(s, t)
    for t in range(stages - 1, -1, -1):
        for s in (2, 3, 0, 1):
            for copy in flying[s]:
                copy.wait()
            if t > 0:
                flying[s] = start_gather(s, t - 1)
    sums_out[...] = whole[...]


def output_kernel(grad_h, sums_h, state_grad, dw_in, db_in, dw_mid, db_mid, dw_out, db_out, grad, sums, load):
    loads = [pltpu.make_async_copy(sums_h, sums, load.at[0]), pltpu.make_async_copy(grad_h, grad, load.at[1])]
    for copy in loads:
        copy.start()
    ne, nz, hid = dw_in.shape
    r_mid, r_out = ne * nz + 16, ne * nz + 16 + ne * hid
    r_b = r_out + ne * nz
    loads[1].wait()
    for i in range(grad.shape[0]):
        state_grad[:, i, :] = grad[i]
    loads[0].wait()
    per = 128 // nz
    for e in range(ne):
        s, at = e // per, (e % per) * nz
        db_out[e:e + 1, :] = sums[s, r_b + 32:r_b + 33, at:at + nz]
        for s in range(2):
            lanes = slice(s * 128, (s + 1) * 128)
            dw_in[e, :, lanes] = sums[s, e * nz:(e + 1) * nz, :]
            dw_mid[e, :, lanes] = sums[s, r_mid + e * hid:r_mid + (e + 1) * hid, :]
            dw_out[e, :, lanes] = sums[s, r_out + e * nz:r_out + (e + 1) * nz, :]
    for s in range(2):
        lanes = slice(s * 128, (s + 1) * 128)
        db_in[:, lanes] = sums[s, ne * nz:ne * nz + ne, :]
        db_mid[:, lanes] = sums[s, r_b + 16:r_b + 16 + ne, :]


def shards(state, cotangent, kappa, labels, drift, w_in, b_in, w_mid, b_mid, w_out, b_out):
    nz, nx, ny = state.shape
    ne, hid, _ = w_in.shape
    n = lax.axis_size("gx")
    bits = n.bit_length() - 1
    rows = ne * nz + ne * hid + ne * nz + 8 * n
    operands = (state, cotangent, kappa, labels, drift[None], jnp.transpose(w_in, (0, 2, 1)), w_mid, w_out,
                b_in, b_mid, b_out)
    chunks, width = nx // rows_per_chunk, rows_per_chunk * ny
    vmem = pl.BlockSpec(memory_space=pltpu.VMEM)
    sds = jax.ShapeDtypeStruct
    grad, sums = pl.pallas_call(
        functools.partial(main_kernel, n),
        out_shape=(sds((nx, nz, ny), f32), sds((2, rows, 128), f32)),
        in_specs=[pl.BlockSpec(memory_space=pltpu.HBM)] * len(operands),
        out_specs=(vmem, vmem),
        scratch_shapes=[pltpu.VMEM(x.shape, x.dtype) for x in operands]
        + [
            pltpu.SemaphoreType.DMA((len(operands),)),
            pltpu.VMEM((2 * hid + nz, 8), f32),
            pltpu.VMEM((hid, ne * nz), bf16),
            pltpu.VMEM((ne * nz, hid), bf16),
            pltpu.VMEM((hid, ne * hid), bf16),
            pltpu.VMEM((hid, ne * hid), bf16),
            pltpu.VMEM((hid, ne * nz), bf16),
            pltpu.VMEM((nx + 2, 3 * nz, ny), f32),
            pltpu.VMEM((nx + 2, 2 * nz, ny), f32),
            pltpu.VMEM((nx, nz, ny), f32),
            pltpu.VMEM((nx, nz, ny), f32),
            pltpu.VMEM((chunks, hid, width), bf16),
            pltpu.VMEM((chunks, hid, width), bf16),
            pltpu.VMEM((chunks, hid, width), f32),
            pltpu.VMEM((chunks, hid, width), f32),
            pltpu.VMEM((2, rows, 128), f32),
            pltpu.VMEM((2, 8, 128), f32),
            pltpu.VMEM((2, n, 8, 128), f32),
        ]
        + [
            pltpu.VMEM((2, rows, 128), f32),
            pltpu.SemaphoreType.DMA((2,)),
            pltpu.SemaphoreType.DMA((2,)),
            pltpu.SemaphoreType.DMA((2,)),
            pltpu.SemaphoreType.DMA((2,)),
            pltpu.SemaphoreType.DMA((2, n)),
            pltpu.SemaphoreType.DMA((2, n)),
            pltpu.SemaphoreType.DMA((4, 2 * bits, 3)),
            pltpu.SemaphoreType.DMA((4, 2 * bits, 3)),
            pltpu.VMEM((2, rows, 128), f32),
        ],
        compiler_params=pltpu.CompilerParams(
            collective_id=0, has_side_effects=True, vmem_limit_bytes=62 * 1024 * 1024),
        name="heun_reverse",
    )(*operands)
    outs = pl.pallas_call(
        output_kernel,
        out_shape=(
            sds((nz, nx, ny), f32), sds((ne, nz, hid), f32), sds((ne, hid), f32),
            sds((ne, hid, hid), f32), sds((ne, hid), f32), sds((ne, nz, hid), f32), sds((ne, nz), f32)),
        in_specs=[pl.BlockSpec(memory_space=pltpu.HBM)] * 2,
        out_specs=(vmem,) * 7,
        scratch_shapes=[pltpu.VMEM(grad.shape, f32), pltpu.VMEM(sums.shape, f32),
                        pltpu.SemaphoreType.DMA((2,))],
        compiler_params=pltpu.CompilerParams(vmem_limit_bytes=62 * 1024 * 1024),
        name="place_outputs",
    )(grad, sums)
    return (outs[0], jnp.transpose(outs[1], (0, 2, 1))) + tuple(outs[2:])


def solution(mesh):
    cells, replicated = P(None, ("parts", "gx"), None), P()
    return jax.shard_map(
        shards,
        mesh=mesh,
        in_specs=(cells, cells, P(("parts", "gx"), None), P(("parts", "gx"), None)) + (replicated,) * 7,
        out_specs=(cells, P("parts", None, None), P("parts", None), P("parts", None, None),
                   P("parts", None), P("parts", None, None), P("parts", None)),
        check_vma=False,
    )
```
